32 devices in a mesh: seq: 8 (over y, x, core), head: 4 (over z).
Axes of the slice: x: 2, y: 2, z: 4, core: 2. Of those that a mesh axis runs over, the one named last changes fastest.
Arguments:
- queries: bfloat16 [8192, 32, 128], P(('seq', 'head')), may hold values from -48 to 48
- keys_in: bfloat16 [8192, 32, 128], P(('seq', 'head')), may hold values from -48 to 48
- values: bfloat16 [8192, 32, 128], P(('seq', 'head')), may hold values from -48 to 48
- cotangent: bfloat16 [8192, 32, 128], P(('seq', 'head')), may hold values from -48 to 48
Outputs:
- attended: bfloat16 [8192, 32, 128], P('seq', 'head')
- grad_queries: bfloat16 [8192, 32, 128], P('seq', 'head')
- grad_keys: bfloat16 [8192, 32, 128], P('seq', 'head')
- grad_values: bfloat16 [8192, 32, 128], P('seq', 'head')
The draws below stay inside these ranges and needn't reach their ends.
All inputs are finite; a program needn't handle non-finite values.
Results may differ from the reference program's by a relative error of at most 0.01.
Values may be sent and summed in bfloat16 or wider, within the bound.
No kernel may reach another device: no remote copies, remote signals or barrier semaphores. Data moves between devices by JAX's collectives and lax.ppermute only.
A program may use at most 128 MiB of HBM per device.

```python
import jax
import jax.numpy as jnp
from jax import lax

HEADS = 32
DH = 128
BLOCK = 512
OFFSET = 1048576
SEQ = 8192


def steps_of(rng, shape, cuts, least, top_value):
    def one(dim, blocks):
        steps = jax.random.uniform(jax.random.fold_in(jax.random.fold_in(rng, 6), dim), (blocks,), jnp.float32, least / len(cuts), top_value / len(cuts))
        return jnp.repeat(jnp.exp(steps), shape[dim] // blocks).reshape((-1,) + (1,) * (len(shape) - dim - 1))

    loudness = one(*cuts[0])
    for cut in cuts[1:]:
        loudness = loudness * one(*cut)
    return loudness


def bell_draw(rng, shape, deviation, bound, cuts=(), kind=jnp.bfloat16):
    gain = steps_of(rng, shape, cuts, -0.22, 0.18) if cuts else 1.0
    values = jax.random.normal(rng, shape, jnp.float32) * deviation * gain
    return jnp.minimum(jnp.maximum(values, -bound), bound).astype(kind)


def setup_inputs(seed: int = 0) -> dict:
    key_of = jax.random.split(jax.random.key(seed), 5)
    queries = bell_draw(key_of[0], (SEQ, HEADS, DH), 8.0, 48.0, ((0, 32),))
    keys_in = bell_draw(key_of[1], (SEQ, HEADS, DH), 8.0, 48.0, ((0, 32),))
    values = bell_draw(key_of[2], (SEQ, HEADS, DH), 8.0, 48.0, ((0, 32),))
    cotangent = bell_draw(key_of[3], (SEQ, HEADS, DH), 8.0, 48.0, ((0, 32),))
    return {"queries": queries, "keys_in": keys_in, "values": values, "cotangent": cotangent}


def reference(queries, keys_in, values, cotangent):
    block_count = SEQ // BLOCK
    position = (jnp.arange(SEQ, dtype=jnp.int32) + OFFSET + 1).astype(jnp.float32)
    scaled_grad = (cotangent.astype(jnp.float32) / position[:, None, None]).astype(jnp.bfloat16)
    causal_mask = jnp.arange(BLOCK)[:, None] >= jnp.arange(BLOCK)[None, :]

    def to_blocks(array):
        return array.reshape(block_count, BLOCK, HEADS, DH)

    sequence_blocks = (to_blocks(queries), to_blocks(keys_in), to_blocks(values), to_blocks(scaled_grad), position.reshape(block_count, BLOCK))

    def masked_scores(left_side, right_side):
        raw_scores = jnp.einsum('thd,shd->hts', left_side, right_side)
        return jnp.where(causal_mask[None], raw_scores, 0.0).astype(jnp.bfloat16).astype(jnp.float32)

    def widen(block_data):
        return [part.astype(jnp.float32) for part in block_data[:4]]

    def forward(carried, block_data):
        query_wide, key_wide, value_wide, grad_wide = widen(block_data)
        state_used = carried.astype(jnp.bfloat16).astype(jnp.float32)
        attention = masked_scores(query_wide, key_wide)
        grad_scores = masked_scores(grad_wide, value_wide)
        result = jnp.einsum('thd,hde->the', query_wide, state_used) + jnp.einsum('hts,she->the', attention, value_wide)
        result = result / block_data[4][:, None, None]
        grad_query = jnp.einsum('the,hde->thd', grad_wide, state_used) + jnp.einsum('hts,shd->thd', grad_scores, key_wide)
        carried = carried + jnp.einsum('shd,she->hde', key_wide, value_wide)
        return carried, (result.astype(jnp.bfloat16), grad_query.astype(jnp.bfloat16))

    def backward(carried, block_data):
        query_wide, key_wide, value_wide, grad_wide = widen(block_data)
        state_used = carried.astype(jnp.bfloat16).astype(jnp.float32)
        attention = masked_scores(query_wide, key_wide)
        grad_scores = masked_scores(grad_wide, value_wide)
        grad_key = jnp.einsum('she,hde->shd', value_wide, state_used) + jnp.einsum('hts,thd->shd', grad_scores, query_wide)
        grad_value = jnp.einsum('shd,hde->she', key_wide, state_used) + jnp.einsum('hts,the->she', attention, grad_wide)
        carried = carried + jnp.einsum('thd,the->hde', query_wide, grad_wide)
        return carried, (grad_key.astype(jnp.bfloat16), grad_value.astype(jnp.bfloat16))

    zero_state = jnp.zeros((HEADS, DH, DH), jnp.float32)
    final_state, (attended, grad_queries) = lax.scan(forward, zero_state, sequence_blocks)
    final_other, (grad_keys, grad_values) = lax.scan(backward, zero_state, sequence_blocks, reverse=True)
    shape_out = (SEQ, HEADS, DH)
    return (attended.reshape(shape_out), grad_queries.reshape(shape_out), grad_keys.reshape(shape_out), grad_values.reshape(shape_out))
```

```python
import functools

import jax
import jax.numpy as jnp
from jax import lax
from jax.experimental import pallas as pl
from jax.experimental.pallas import tpu as pltpu
from jax.sharding import PartitionSpec as P

BLOCK = 256
OFFSET = 1048576
PAIR = 2
F32 = jnp.float32
BF16 = jnp.bfloat16
ANY = pl.BlockSpec(memory_space=pl.ANY)
VMEM = pl.BlockSpec(memory_space=pltpu.VMEM)
SMEM = pl.BlockSpec(memory_space=pltpu.SMEM)
VMEM_BYTES = 48 * 1024 * 1024


def dot(a, b, ca, cb):
    return lax.dot_general(a, b, (((ca,), (cb,)), ((), ())), preferred_element_type=F32)


def params():
    return pltpu.CompilerParams(vmem_limit_bytes=VMEM_BYTES)


def cost(flops, nbytes):
    return pl.CostEstimate(flops=int(flops), bytes_accessed=int(nbytes), transcendentals=0)


def partner(z, d):
    return z ^ d


def position(first, rows, width):
    index = lax.broadcasted_iota(jnp.int32, (rows, width), 0) + (first + OFFSET + 1)
    return index.astype(F32)


def pack_kernel(where, *refs, n, scale, n_after):
    sources, rest = refs[: 2 * n], refs[2 * n + n_after :]
    outs, wide = rest[:n], rest[n]
    rows, width = outs[0].shape[2:]
    for d in range(n):
        for a in range(2):
            rows_of_both = sources[2 * d + a][...].reshape(PAIR * rows, width).astype(F32)
            wide[...] = rows_of_both
            for h in range(PAIR):
                part = wide[pl.ds(h, rows, stride=PAIR), :]
                if scale and a == 1:
                    part = part / position((where[0] * n + where[1]) * rows, rows, width)
                outs[d][a, h] = part.astype(BF16)


def pack(where, first, second, chunk, n, scale, after):
    rows, pair_count, _, width = first.shape
    per_group = pair_count // n

    def spec(d):
        return pl.BlockSpec(
            (rows, 1, PAIR, width),
            lambda i, w: (0, partner(w[1], d) * per_group + chunk, 0, 0),
        )

    out = jax.ShapeDtypeStruct((2, PAIR, rows, width), BF16)
    specs = [spec(d) for d in range(n) for _ in range(2)] + [ANY] * len(after)
    operands = [x for _ in range(n) for x in (first, second)] + list(after)
    return pl.pallas_call(
        functools.partial(pack_kernel, n=n, scale=scale, n_after=len(after)),
        grid_spec=pltpu.PrefetchScalarGridSpec(
            num_scalar_prefetch=1,
            grid=(1,),
            in_specs=specs,
            out_specs=[pl.BlockSpec((2, PAIR, rows, width), lambda i, w: (0, 0, 0, 0))] * n,
            scratch_shapes=[pltpu.VMEM((PAIR * rows, width), F32)],
        ),
        out_shape=[out] * n,
        compiler_params=params(),
        cost_estimate=cost(0, 8 * n * PAIR * rows * width),
    )(where, *operands)


def exchange(pieces, n):
    received = [pieces[0]]
    for d in range(1, n):
        received.append(None)
    for d in reversed(range(1, n)):
        received[d] = lax.ppermute(pieces[d], "head", [(j, j ^ d) for j in range(n)])
    return received


def state_kernel(*refs, n):
    for h in range(PAIR):
        total = dot(refs[0][0, h], refs[0][1, h], 0, 0)
        for d in range(1, n):
            total = total + dot(refs[d][0, h], refs[d][1, h], 0, 0)
        refs[n][h] = total.astype(BF16)


def shard_state(pieces):
    n = len(pieces)
    _, _, rows, width = pieces[0].shape
    return pl.pallas_call(
        functools.partial(state_kernel, n=n),
        in_specs=[VMEM] * n,
        out_specs=VMEM,
        out_shape=jax.ShapeDtypeStruct((PAIR, width, width), BF16),
        compiler_params=params(),
        cost_estimate=cost(2 * n * PAIR * rows * width * width, 4 * n * PAIR * rows * width),
    )(*pieces)


def chunk_kernel(where, *refs, n, block):
    kv_pieces, qg_pieces = refs[:n], refs[n : 2 * n]
    kv_states, qg_states = refs[2 * n], refs[2 * n + 1]
    result, grad_query, grad_key, grad_value = refs[-8:-4]
    left, right, wide, used = refs[-4:]
    shard_count = kv_states.shape[0]
    rows, width = kv_pieces[0].shape[2:]
    row_count = n * rows
    block_count = row_count // block
    me, z = where[0], where[1]
    for d in range(n):
        start = pl.multiple_of(partner(z, d) * rows, rows)
        left[:, :, pl.ds(start, rows), :] = kv_pieces[d][...]
        right[:, :, pl.ds(start, rows), :] = qg_pieces[d][...]
    causal = lax.broadcasted_iota(jnp.int32, (block, block), 0) >= lax.broadcasted_iota(
        jnp.int32, (block, block), 1
    )

    def scores(a, b):
        return jnp.where(causal, dot(a, b, 1, 1), 0.0).astype(BF16)

    for h in range(PAIR):
        before = jnp.zeros((width, width), F32)
        after = jnp.zeros((width, width), F32)
        for j in range(shard_count):
            before = before + jnp.where(j < me, kv_states[j, h].astype(F32), 0.0)
            after = after + jnp.where(j > me, qg_states[j, h].astype(F32), 0.0)
        for b in reversed(range(block_count)):
            span = pl.ds(b * block, block)
            used[b] = after.astype(BF16)
            if b:
                after = after + dot(right[0, h, span], right[1, h, span], 0, 0)
        for b in range(block_count):
            span = pl.ds(b * block, block)
            key, value = left[0, h, span], left[1, h, span]
            query, grad = right[0, h, span], right[1, h, span]
            prefix, suffix = before.astype(BF16), used[b]
            attention, grad_scores = scores(query, key), scores(grad, value)
            out_rows = pl.ds(b * block * PAIR + h, block, stride=PAIR)
            wide[0, out_rows, :] = (
                dot(query, prefix, 1, 0) + dot(attention, value, 1, 0)
            ) / position(me * row_count + b * block, block, width)
            wide[1, out_rows, :] = dot(grad, prefix, 1, 1) + dot(grad_scores, key, 1, 0)
            wide[2, out_rows, :] = dot(value, suffix, 1, 1) + dot(grad_scores, query, 0, 0)
            wide[3, out_rows, :] = dot(key, suffix, 1, 0) + dot(attention, grad, 0, 0)
            if b + 1 < block_count:
                before = before + dot(key, value, 0, 0)
    for i, out in enumerate((result, grad_query, grad_key, grad_value)):
        out[...] = wide[i].astype(BF16).reshape(row_count, 1, PAIR, width)


def compute_chunk(where, kv, qg, kv_states, qg_states, outs, chunk, pair_count):
    n = len(kv)
    _, _, rows, width = kv[0].shape
    row_count = n * rows
    block = min(BLOCK, row_count)
    whole = jax.ShapeDtypeStruct((row_count, pair_count, PAIR, width), BF16)
    piece = pl.BlockSpec((2, PAIR, rows, width), lambda i, w: (0, 0, 0, 0))
    state = pl.BlockSpec(kv_states.shape, lambda i, w: (0, 0, 0, 0))
    held = [] if outs is None else list(outs)
    first_held = 1 + 2 * n + 2
    flops = PAIR * row_count * width * (12 * block + 12 * width)
    return pl.pallas_call(
        functools.partial(chunk_kernel, n=n, block=block),
        grid_spec=pltpu.PrefetchScalarGridSpec(
            num_scalar_prefetch=1,
            grid=(1,),
            in_specs=[piece] * (2 * n) + [state] * 2 + [ANY] * len(held),
            out_specs=[
                pl.BlockSpec((row_count, 1, PAIR, width), lambda i, w: (0, chunk, 0, 0))
            ]
            * 4,
            scratch_shapes=[
                pltpu.VMEM((2, PAIR, row_count, width), BF16),
                pltpu.VMEM((2, PAIR, row_count, width), BF16),
                pltpu.VMEM((4, row_count * PAIR, width), F32),
                pltpu.VMEM((row_count // block, width, width), BF16),
            ],
        ),
        out_shape=[whole] * 4,
        input_output_aliases={first_held + i: i for i in range(len(held))},
        compiler_params=params(),
        cost_estimate=cost(flops, 16 * PAIR * row_count * width),
    )(where, *kv, *qg, kv_states, qg_states, *held)


def shards(queries, keys_in, values, cotangent):
    n = lax.axis_size("head")
    rows, head_count, width = queries.shape
    pair_count = head_count // PAIR
    per_group = pair_count // n
    where = jnp.stack([lax.axis_index("seq"), lax.axis_index("head")]).astype(jnp.int32)

    def paired(x):
        return x.reshape(rows, pair_count, PAIR, width)

    queries, keys_in, values, cotangent = map(paired, (queries, keys_in, values, cotangent))
    arrived = []
    for unit in range(2 * per_group):
        after = arrived[unit - 2][1:] if unit >= 2 else []
        pieces = (
            pack(where, keys_in, values, unit // 2, n, False, after)
            if unit % 2 == 0
            else pack(where, queries, cotangent, unit // 2, n, True, after)
        )
        arrived.append(exchange(pieces, n))
    outs = None
    for chunk in range(per_group):
        kv, qg = arrived[2 * chunk], arrived[2 * chunk + 1]
        kv_states = lax.all_gather(shard_state(kv), "seq", axis=0)
        qg_states = lax.all_gather(shard_state(qg), "seq", axis=0)
        outs = compute_chunk(where, kv, qg, kv_states, qg_states, outs, chunk, per_group)
    return tuple(x.reshape(n * rows, per_group * PAIR, width) for x in outs)


def solution(mesh):
    rows_spec = P(("seq", "head"), None, None)
    heads_spec = P("seq", "head", None)
    return jax.shard_map(
        shards, mesh=mesh, in_specs=(rows_spec,) * 4, out_specs=(heads_spec,) * 4, check_vma=False
    )
```

```python
import functools

import jax
import jax.numpy as jnp
from jax import lax
from jax.experimental import pallas as pl
from jax.experimental.pallas import tpu as pltpu
from jax.sharding import PartitionSpec as P

BLOCK = 256
OFFSET = 1048576
PAIR = 2
F32 = jnp.float32
BF16 = jnp.bfloat16
ANY = pl.BlockSpec(memory_space=pl.ANY)
HBM = pl.BlockSpec(memory_space=pltpu.HBM)
VMEM = pl.BlockSpec(memory_space=pltpu.VMEM)
SMEM = pl.BlockSpec(memory_space=pltpu.SMEM)
VMEM_BYTES = 32 * 1024 * 1024


def dot(a, b, ca, cb):
    return lax.dot_general(a, b, (((ca,), (cb,)), ((), ())), preferred_element_type=F32)


def params():
    return pltpu.CompilerParams(vmem_limit_bytes=VMEM_BYTES)


def cost(flops, nbytes):
    return pl.CostEstimate(flops=int(flops), bytes_accessed=int(nbytes), transcendentals=0)


def position(first, rows, width):
    index = lax.broadcasted_iota(jnp.int32, (rows, width), 0) + (first + OFFSET + 1)
    return index.astype(F32)


def head_rows(both, wide, h):
    rows, _, width = both.shape
    if h == 0:
        wide[...] = both.reshape(PAIR * rows, width).astype(F32)
    return wide[pl.ds(h, rows, stride=PAIR), :]


def fetch_pairs(where, arrays, held, sems, n, chunk):
    per_group = arrays[0].shape[1] // n
    copies = []
    for d in range(n):
        pair = (where[1] ^ d) * per_group + chunk
        for a, x in enumerate(arrays):
            copies.append(pltpu.make_async_copy(x.at[:, pair], held.at[d, a], sems.at[d, a]))
    for c in copies:
        c.start()
    return copies


def pack_kernel(where, *refs, n, scales, chunk):
    count = len(scales)
    arrays, outs = refs[:count], refs[-3 - n : -3]
    held, wide, sems = refs[-3:]
    rows, width = outs[0].shape[2:]
    copies = fetch_pairs(where, arrays, held, sems, n, chunk)
    for d in range(n):
        for a, scale in enumerate(scales):
            copies[d * count + a].wait()
            for h in range(PAIR):
                part = head_rows(held[d, a], wide, h)
                if scale:
                    part = part / position((where[0] * n + where[1]) * rows, rows, width)
                outs[d][a, h] = part.astype(BF16)


def pack(where, arrays, scales, chunk, n, after):
    rows, _, _, width = arrays[0].shape
    count = len(arrays)
    return pl.pallas_call(
        functools.partial(pack_kernel, n=n, scales=scales, chunk=chunk),
        in_specs=[SMEM] + [HBM] * count + [ANY] * len(after),
        out_specs=[VMEM] * n,
        out_shape=[jax.ShapeDtypeStruct((count, PAIR, rows, width), BF16)] * n,
        scratch_shapes=[
            pltpu.VMEM((n, count, rows, PAIR, width), BF16),
            pltpu.VMEM((PAIR * rows, width), F32),
            pltpu.SemaphoreType.DMA((n, count)),
        ],
        compiler_params=params(),
        cost_estimate=cost(0, 4 * count * n * PAIR * rows * width),
    )(where, *arrays, *after)


def exchange(pieces, n):
    received = list(pieces)
    for d in reversed(range(1, n)):
        received[d] = lax.ppermute(pieces[d], "head", [(j, j ^ d) for j in range(n)])
    return received


def own_rows_kernel(where, *refs, n, chunk):
    arrays, outs = refs[:2], refs[-4 - n : -4]
    held, wide, parts, sems = refs[-4:]
    rows, width = held.shape[2], held.shape[4]
    copies = fetch_pairs(where, arrays, held, sems, n, chunk)
    for d in range(n):
        for a in range(2):
            copies[2 * d + a].wait()
            for h in range(PAIR):
                part = head_rows(held[d, a], wide, h)
                if a == 1:
                    part = part / position((where[0] * n + where[1]) * rows, rows, width)
                parts[a, h] = part.astype(BF16)
        for h in range(PAIR):
            outs[d][h] = dot(parts[0, h], parts[1, h], 0, 0).astype(BF16)


def own_rows_state(where, queries, cotangent, chunk, n, after):
    rows, _, _, width = queries.shape
    return pl.pallas_call(
        functools.partial(own_rows_kernel, n=n, chunk=chunk),
        in_specs=[SMEM] + [HBM] * 2 + [ANY] * len(after),
        out_specs=[VMEM] * n,
        out_shape=[jax.ShapeDtypeStruct((PAIR, width, width), BF16)] * n,
        scratch_shapes=[
            pltpu.VMEM((n, 2, rows, PAIR, width), BF16),
            pltpu.VMEM((PAIR * rows, width), F32),
            pltpu.VMEM((2, PAIR, rows, width), BF16),
            pltpu.SemaphoreType.DMA((n, 2)),
        ],
        compiler_params=params(),
        cost_estimate=cost(2 * n * PAIR * rows * width * width, 8 * n * PAIR * rows * width),
    )(where, queries, cotangent, *after)


def sum_to_group(parts, n):
    parts, bit = list(parts), 1
    while bit < n:
        for d in range(0, n, 2 * bit):
            came = lax.ppermute(parts[d + bit], "head", [(j, j ^ bit) for j in range(n)])
            parts[d] = (parts[d].astype(F32) + came.astype(F32)).astype(BF16)
        bit *= 2
    return parts[0]


def state_kernel(*refs, n, sides):
    for i in range(sides):
        pieces = refs[i * n : (i + 1) * n]
        for h in range(PAIR):
            total = dot(pieces[0][0, h], pieces[0][1, h], 0, 0)
            for d in range(1, n):
                total = total + dot(pieces[d][0, h], pieces[d][1, h], 0, 0)
            refs[-1][i * PAIR + h] = total.astype(BF16)


def shard_state(*sides):
    n = len(sides[0])
    _, _, rows, width = sides[0][0].shape
    count = len(sides)
    return pl.pallas_call(
        functools.partial(state_kernel, n=n, sides=count),
        in_specs=[VMEM] * (n * count),
        out_specs=VMEM,
        out_shape=jax.ShapeDtypeStruct((PAIR * count, width, width), BF16),
        compiler_params=params(),
        cost_estimate=cost(
            2 * count * n * PAIR * rows * width * width, 4 * count * n * PAIR * rows * width
        ),
    )(*[p for side in sides for p in side])


def chunk_kernel(where, *refs, n, block, chunk, slots, n_refs, n_outs, want):
    pieces, kv_states, qg_states = refs[:n_refs], refs[n_refs], refs[n_refs + 1]
    outs = refs[-8 - n_outs : -8]
    held, wide, stage, sums, before_used, after_used, in_sems, out_sems = refs[-8:]
    rows, width = pieces[0].shape[2:]
    row_count = n * rows
    block_count = row_count // block
    shard_count = kv_states.shape[0]
    me, z = where[0], where[1]
    copies = []
    for i, (first, a) in enumerate(slots):
        for d in range(n):
            start = pl.multiple_of((z ^ d) * rows, rows)
            copies.append(
                pltpu.make_async_copy(
                    pieces[first + d].at[a],
                    held.at[i, :, pl.ds(start, rows), :],
                    in_sems.at[i, d],
                )
            )
    for c in copies:
        c.start()

    late = "grads" in want

    def add_shards(j, _):
        for h in range(PAIR):
            sums[0, h] += jnp.where(j < me, kv_states[j, h].astype(F32), 0.0)
            if late:
                sums[1, h] += jnp.where(j > me, qg_states[j, h].astype(F32), 0.0)
        return 0

    sums[...] = jnp.zeros_like(sums)
    lax.fori_loop(0, shard_count, add_shards, 0)
    for c in copies:
        c.wait()

    def span(b):
        return pl.ds(pl.multiple_of(b * block, block), block)

    def add_blocks(i, _):
        last = block_count - 1 - i
        for h in range(PAIR):
            before_used[i, h] = sums[0, h].astype(BF16)
            sums[0, h] += dot(held[0, h, span(i)], held[1, h, span(i)], 0, 0)
            if late:
                after_used[last, h] = sums[1, h].astype(BF16)
                sums[1, h] += dot(held[2, h, span(last)], held[3, h, span(last)], 0, 0)
        return 0

    lax.fori_loop(0, block_count, add_blocks, 0)
    causal = lax.broadcasted_iota(jnp.int32, (block, block), 0) >= lax.broadcasted_iota(
        jnp.int32, (block, block), 1
    )

    def scores(a, b):
        return jnp.where(causal, dot(a, b, 1, 1), 0.0).astype(BF16)

    def out_copy(i, b):
        return pltpu.make_async_copy(
            stage.at[i, span(b)], outs[i].at[span(b), chunk], out_sems.at[i, b]
        )

    def one_block(b, _):
        at = span(b)
        for h in range(PAIR):
            key, value, query = held[0, h, at], held[1, h, at], held[2, h, at]
            prefix = before_used[b, h]
            mine = pl.ds(h, block, stride=PAIR)
            attention = scores(query, key)
            i = 0
            if "attended" in want:
                result = dot(query, prefix, 1, 0) + dot(attention, value, 1, 0)
                wide[0, mine, :] = result / position(me * row_count + b * block, block, width)
                i = 1
            if late:
                grad, suffix = held[3, h, at], after_used[b, h]
                grad_scores = scores(grad, value)
                wide[i, mine, :] = dot(grad, prefix, 1, 1) + dot(grad_scores, key, 1, 0)
                wide[i + 1, mine, :] = dot(value, suffix, 1, 1) + dot(grad_scores, query, 0, 0)
                wide[i + 2, mine, :] = dot(key, suffix, 1, 0) + dot(attention, grad, 0, 0)
        for i in range(n_outs):
            stage[i, at] = wide[i].astype(BF16).reshape(block, PAIR, width)
            out_copy(i, b).start()
        return 0

    lax.fori_loop(0, block_count, one_block, 0)

    def finish(b, _):
        for i in range(n_outs):
            out_copy(i, b).wait()
        return 0

    lax.fori_loop(0, block_count, finish, 0)


def compute_chunk(where, units, slots, kv_states, qg_states, outs, chunk, pair_count, want):
    n = len(units[0])
    _, _, rows, width = units[0][0].shape
    row_count = n * rows
    block = min(BLOCK, row_count)
    block_count = row_count // block
    whole = jax.ShapeDtypeStruct((row_count, pair_count, PAIR, width), BF16)
    n_outs = ("attended" in want) + 3 * ("grads" in want)
    held = [] if outs is None else list(outs)
    pieces = [p for unit in units for p in unit]
    flops = PAIR * row_count * width * 3 * n_outs * (block + width)
    return pl.pallas_call(
        functools.partial(
            chunk_kernel,
            n=n,
            block=block,
            chunk=chunk,
            slots=[(n * u, a) for u, a in slots],
            n_refs=len(pieces),
            n_outs=n_outs,
            want=want,
        ),
        in_specs=[SMEM] + [ANY] * len(pieces) + [VMEM] * 2 + [HBM] * len(held),
        out_specs=[HBM] * n_outs,
        out_shape=[whole] * n_outs,
        scratch_shapes=[
            pltpu.VMEM((len(slots), PAIR, row_count, width), BF16),
            pltpu.VMEM((n_outs, block * PAIR, width), F32),
            pltpu.VMEM((n_outs, row_count, PAIR, width), BF16),
            pltpu.VMEM((2, PAIR, width, width), F32),
            pltpu.VMEM((block_count, PAIR, width, width), BF16),
            pltpu.VMEM((block_count, PAIR, width, width), BF16),
            pltpu.SemaphoreType.DMA((len(slots), n)),
            pltpu.SemaphoreType.DMA((n_outs, block_count)),
        ],
        input_output_aliases={1 + len(pieces) + 2 + i: i for i in range(len(held))},
        compiler_params=params(),
        cost_estimate=cost(flops, 4 * n_outs * PAIR * row_count * width),
    )(where, *pieces, kv_states, qg_states, *held)


def shards(queries, keys_in, values, cotangent):
    n = lax.axis_size("head")
    rows, head_count, width = queries.shape
    pair_count = head_count // PAIR
    per_group = pair_count // n
    last = per_group - 1
    where = jnp.stack([lax.axis_index("seq"), lax.axis_index("head")]).astype(jnp.int32)
    queries, keys_in, values, cotangent = (
        x.reshape(rows, pair_count, PAIR, width) for x in (queries, keys_in, values, cotangent)
    )
    order = []
    for chunk in range(per_group):
        order += [("kv", chunk), ("qg", chunk)]
    order = order[:-1]
    if per_group > 1:
        order[-2], order[-1] = order[-1], order[-2]
    order += [("q", last), ("g", last)]
    content = {
        "kv": ((keys_in, values), (False, False)),
        "qg": ((queries, cotangent), (False, True)),
        "q": ((queries,), (False,)),
        "g": ((cotangent,), (True,)),
    }
    sent, arrived = [], {}
    for unit, (kind, chunk) in enumerate(order):
        after = arrived[order[unit - 2]][1:] if unit >= 2 else []
        arrays, scales = content[kind]
        sent.append(pack(where, arrays, scales, chunk, n, after))
        arrived[kind, chunk] = exchange(sent[-1], n)
    ahead = own_rows_state(where, queries, cotangent, last, n, sent[1][:1])
    last_qg_states = lax.all_gather(sum_to_group(ahead, n), "seq", axis=0)
    last_kv_states = lax.all_gather(shard_state(arrived["kv", last]), "seq", axis=0)
    outs = None
    both = ("attended", "grads")
    for chunk in range(last):
        kv, qg = arrived["kv", chunk], arrived["qg", chunk]
        states = lax.all_gather(shard_state(kv, qg), "seq", axis=0)
        slots = ((0, 0), (0, 1), (1, 0), (1, 1))
        outs = compute_chunk(
            where, (kv, qg), slots, states[:, :PAIR], states[:, PAIR:], outs, chunk, per_group, both
        )
    kv, q, g = arrived["kv", last], arrived["q", last], arrived["g", last]
    attended = compute_chunk(
        where,
        (kv, q),
        ((0, 0), (0, 1), (1, 0)),
        last_kv_states,
        last_qg_states,
        outs and outs[:1],
        last,
        per_group,
        both[:1],
    )
    grads = compute_chunk(
        where,
        (kv, q, g),
        ((0, 0), (0, 1), (1, 0), (2, 0)),
        last_kv_states,
        last_qg_states,
        outs and outs[1:],
        last,
        per_group,
        both[1:],
    )
    return tuple(x.reshape(n * rows, per_group * PAIR, width) for x in (*attended, *grads))


def solution(mesh):
    rows_spec = P(("seq", "head"), None, None)
    heads_spec = P("seq", "head", None)
    return jax.shard_map(
        shards, mesh=mesh, in_specs=(rows_spec,) * 4, out_specs=(heads_spec,) * 4, check_vma=False
    )
```

```python
import functools

import jax
import jax.numpy as jnp
from jax import lax
from jax.experimental import pallas as pl
from jax.experimental.pallas import tpu as pltpu
from jax.sharding import PartitionSpec as P

BLOCK = 256
OFFSET = 1048576
PAIR = 2
K, V, Q, G = range(4)
F32 = jnp.float32
BF16 = jnp.bfloat16
ANY = pl.BlockSpec(memory_space=pl.ANY)
HBM = pl.BlockSpec(memory_space=pltpu.HBM)
VMEM = pl.BlockSpec(memory_space=pltpu.VMEM)
SMEM = pl.BlockSpec(memory_space=pltpu.SMEM)
VMEM_BYTES = 32 * 1024 * 1024
TOKEN = jax.ShapeDtypeStruct((8, 128), F32)


def dot(a, b, ca, cb):
    return lax.dot_general(a, b, (((ca,), (cb,)), ((), ())), preferred_element_type=F32)


def params():
    return pltpu.CompilerParams(vmem_limit_bytes=VMEM_BYTES)


def cost(flops, nbytes):
    return pl.CostEstimate(flops=int(flops), bytes_accessed=int(nbytes), transcendentals=0)


def position(first, rows, width):
    index = lax.broadcasted_iota(jnp.int32, (rows, width), 0) + (first + OFFSET + 1)
    return index.astype(F32)


def each(count, body):
    def step(i, _):
        body(i)
        return 0

    lax.fori_loop(0, count, step, 0)


def fetch_pairs(where, arrays, items, held, sems, n):
    per_group = arrays[0].shape[1] // n
    copies = []
    for d in range(n):
        for i, (a, chunk) in enumerate(items):
            pair = (where[1] ^ d) * per_group + chunk
            copies.append(
                pltpu.make_async_copy(arrays[a].at[:, pair], held.at[d, i], sems.at[d, i])
            )
    for c in copies:
        c.start()
    for c in copies:
        c.wait()


def split_heads(where, items, held, wide, put, d, n):
    rows, width = held.shape[2], held.shape[4]
    plain = sum(a != G for a, _ in items)

    def some(first, count, scale):
        def one(j):
            i = first + j
            wide[...] = held[d, i].reshape(PAIR * rows, width).astype(F32)
            for h in range(PAIR):
                part = wide[pl.ds(h, rows, stride=PAIR), :]
                if scale:
                    part = part / position((where[0] * n + where[1]) * rows, rows, width)
                put(i, h, part.astype(BF16))

        if count:
            each(count, one)

    some(0, plain, False)
    some(plain, len(items) - plain, True)


def pack_kernel(where, *refs, n, items):
    arrays, outs = refs[:4], refs[-5 - n : -5]
    held, wide, staged, sems, out_sems = refs[-5:]
    fetch_pairs(where, arrays, items, held, sems, n)

    def one(d):
        def put(i, h, part):
            staged[d, i, h] = part

        split_heads(where, items, held, wide, put, d, n)

    each(n, one)
    copies = [pltpu.make_async_copy(staged.at[d], outs[d], out_sems.at[d]) for d in range(n)]
    for c in copies:
        c.start()
    for c in copies:
        c.wait()


def pack(where, arrays, items, n, after):
    rows, _, _, width = arrays[0].shape
    count = len(items)
    return pl.pallas_call(
        functools.partial(pack_kernel, n=n, items=items),
        in_specs=[SMEM] + [HBM] * 4 + [ANY] * len(after),
        out_specs=[VMEM] * n,
        out_shape=[jax.ShapeDtypeStruct((count, PAIR, rows, width), BF16)] * n,
        scratch_shapes=[
            pltpu.VMEM((n, count, rows, PAIR, width), BF16),
            pltpu.VMEM((PAIR * rows, width), F32),
            pltpu.VMEM((n, count, PAIR, rows, width), BF16),
            pltpu.SemaphoreType.DMA((n, count)),
            pltpu.SemaphoreType.DMA((n,)),
        ],
        compiler_params=params(),
        cost_estimate=cost(0, 4 * count * n * PAIR * rows * width),
    )(where, *arrays, *after)


def exchange(pieces, n):
    received = list(pieces)
    for d in reversed(range(1, n)):
        received[d] = lax.ppermute(pieces[d], "head", [(j, j ^ d) for j in range(n)])
    return received


def own_rows_kernel(where, *refs, n, items):
    arrays, outs = refs[:4], refs[-5 - n : -5]
    held, wide, parts, totals, sems = refs[-5:]
    fetch_pairs(where, arrays, items, held, sems, n)

    def one(d):
        def put(i, h, part):
            parts[i, h] = part

        split_heads(where, items, held, wide, put, d, n)
        for h in range(PAIR):
            totals[d, h] = dot(parts[0, h], parts[1, h], 0, 0).astype(BF16)
            totals[d, PAIR + h] = dot(parts[2, h], parts[3, h], 0, 0).astype(BF16)

    each(n, one)
    for d in range(n):
        outs[d][...] = totals[d]


def own_rows_states(where, arrays, chunk, n, after):
    rows, _, _, width = arrays[0].shape
    items = [(K, chunk), (V, chunk), (Q, chunk), (G, chunk)]
    return pl.pallas_call(
        functools.partial(own_rows_kernel, n=n, items=items),
        in_specs=[SMEM] + [HBM] * 4 + [ANY] * len(after),
        out_specs=[VMEM] * n,
        out_shape=[jax.ShapeDtypeStruct((2 * PAIR, width, width), BF16)] * n,
        scratch_shapes=[
            pltpu.VMEM((n, 4, rows, PAIR, width), BF16),
            pltpu.VMEM((PAIR * rows, width), F32),
            pltpu.VMEM((4, PAIR, rows, width), BF16),
            pltpu.VMEM((n, 2 * PAIR, width, width), BF16),
            pltpu.SemaphoreType.DMA((n, 4)),
        ],
        compiler_params=params(),
        cost_estimate=cost(4 * n * PAIR * rows * width * width, 16 * n * PAIR * rows * width),
    )(where, *arrays, *after)


def sum_to_group(parts, n):
    parts, bit = list(parts), 1
    while bit < n:
        for d in range(0, n, 2 * bit):
            came = lax.ppermute(parts[d + bit], "head", [(j, j ^ bit) for j in range(n)])
            parts[d] = (parts[d].astype(F32) + came.astype(F32)).astype(BF16)
        bit *= 2
    return parts[0]


def state_kernel(*refs, n, sides):
    out = refs[-1]

    def one(h):
        for i, (first, a, second, b) in enumerate(sides):
            total = dot(refs[first][a, h], refs[second][b, h], 0, 0)
            for d in range(1, n):
                total = total + dot(refs[first + d][a, h], refs[second + d][b, h], 0, 0)
            out[i * PAIR + h] = total.astype(BF16)

    each(PAIR, one)


def shard_states(units, sides, after):
    n = len(units[0])
    _, _, rows, width = units[0][0].shape
    count = len(sides)
    return pl.pallas_call(
        functools.partial(state_kernel, n=n, sides=[(n * u, a, n * w, b) for u, a, w, b in sides]),
        in_specs=[VMEM] * (n * len(units)) + [ANY] * len(after),
        out_specs=VMEM,
        out_shape=jax.ShapeDtypeStruct((PAIR * count, width, width), BF16),
        compiler_params=params(),
        cost_estimate=cost(
            2 * count * n * PAIR * rows * width * width, 4 * count * n * PAIR * rows * width
        ),
    )(*[p for unit in units for p in unit], *after)


def place_rows(z, pieces, places, held, first, sems, n):
    rows = pieces[0].shape[2]
    copies = []
    for i, (at, a) in enumerate(places):
        for d in range(n):
            start = pl.multiple_of((z ^ d) * rows, rows)
            copies.append(
                pltpu.make_async_copy(
                    pieces[at + d].at[a],
                    held.at[first + i, :, pl.ds(start, rows), :],
                    sems.at[i, d],
                )
            )
    for c in copies:
        c.start()
    return copies


def masks(block):
    row = lax.broadcasted_iota(jnp.int32, (block, block), 0)
    column = lax.broadcasted_iota(jnp.int32, (block, block), 1)
    return row >= column, row <= column


def scores(a, b, mask):
    return jnp.where(mask, dot(a, b, 1, 1), 0.0).astype(BF16)


def span(b, block):
    return pl.ds(b * block if isinstance(b, int) else pl.multiple_of(b * block, block), block)


def add_shards(me, kv_states, qg_states, sums):
    sums[...] = jnp.zeros_like(sums)

    def one(j):
        for h in range(PAIR):
            sums[0, h] += jnp.where(j < me, kv_states[j, h].astype(F32), 0.0)
            sums[1, h] += jnp.where(j > me, qg_states[j, h].astype(F32), 0.0)

    each(kv_states.shape[0], one)


def out_copy(stage, outs, sems, i, b, block, chunk):
    at = span(b, block)
    return pltpu.make_async_copy(stage.at[i, at], outs[i].at[at, chunk], sems.at[i, b])


def send_block(wide, stage, outs, sems, b, block, chunk, width):
    for i in range(len(outs)):
        stage[i, span(b, block)] = wide[i].astype(BF16).reshape(block, PAIR, width)
        out_copy(stage, outs, sems, i, b, block, chunk).start()


def chunk_kernel(where, *refs, n, block, chunk, slots, n_pieces):
    pieces, kv_states, qg_states = refs[:n_pieces], refs[n_pieces], refs[n_pieces + 1]
    outs, token = refs[-13:-9], refs[-9]
    held, wide, stage, sums, before_used, after_used, in_sems, out_sems = refs[-8:]
    row_count, width = held.shape[2:]
    block_count = row_count // block
    me, z = where[0], where[1]
    copies = place_rows(z, pieces, slots, held, 0, in_sems, n)
    add_shards(me, kv_states, qg_states, sums)
    for c in copies:
        c.wait()

    def add_blocks(i):
        last = block_count - 1 - i
        first_at, last_at = span(i, block), span(last, block)
        for h in range(PAIR):
            before_used[i, h] = sums[0, h].astype(BF16)
            sums[0, h] += dot(held[K, h, first_at], held[V, h, first_at], 0, 0)
            after_used[last, h] = sums[1, h].astype(BF16)
            sums[1, h] += dot(held[Q, h, last_at], held[G, h, last_at], 0, 0)

    each(block_count, add_blocks)
    lower, upper = masks(block)

    def one_block(b):
        at = span(b, block)
        for h in range(PAIR):
            key, value = held[K, h, at], held[V, h, at]
            query, grad = held[Q, h, at], held[G, h, at]
            prefix, suffix = before_used[b, h], after_used[b, h]
            mine = pl.ds(h, block, stride=PAIR)
            attention, attention_t = scores(query, key, lower), scores(key, query, upper)
            grad_scores, grad_scores_t = scores(grad, value, lower), scores(value, grad, upper)
            result = dot(query, prefix, 1, 0) + dot(attention, value, 1, 0)
            wide[0, mine, :] = result / position(me * row_count + b * block, block, width)
            wide[1, mine, :] = dot(grad, prefix, 1, 1) + dot(grad_scores, key, 1, 0)
            wide[2, mine, :] = dot(value, suffix, 1, 1) + dot(grad_scores_t, query, 1, 0)
            wide[3, mine, :] = dot(key, suffix, 1, 0) + dot(attention_t, grad, 1, 0)
        send_block(wide, stage, outs, out_sems, b, block, chunk, width)

    each(block_count, one_block)
    token[...] = jnp.zeros_like(token)

    def finish(b):
        for i in range(4):
            out_copy(stage, outs, out_sems, i, b, block, chunk).wait()

    each(block_count, finish)


def compute_chunk(where, units, slots, kv_states, qg_states, outs, chunk, pair_count, after):
    n = len(units[0])
    _, _, rows, width = units[0][0].shape
    row_count = n * rows
    block = min(BLOCK, row_count)
    block_count = row_count // block
    whole = jax.ShapeDtypeStruct((row_count, pair_count, PAIR, width), BF16)
    held = [] if outs is None else list(outs)
    pieces = [p for unit in units for p in unit]
    result = pl.pallas_call(
        functools.partial(
            chunk_kernel,
            n=n,
            block=block,
            chunk=chunk,
            slots=[(n * u, a) for u, a in slots],
            n_pieces=len(pieces),
        ),
        in_specs=[SMEM] + [ANY] * len(pieces) + [VMEM] * 2 + [HBM] * len(held) + [ANY] * len(after),
        out_specs=[HBM] * 4 + [VMEM],
        out_shape=[whole] * 4 + [TOKEN],
        scratch_shapes=[
            pltpu.VMEM((4, PAIR, row_count, width), BF16),
            pltpu.VMEM((4, block * PAIR, width), F32),
            pltpu.VMEM((4, row_count, PAIR, width), BF16),
            pltpu.VMEM((2, PAIR, width, width), F32),
            pltpu.VMEM((block_count, PAIR, width, width), BF16),
            pltpu.VMEM((block_count, PAIR, width, width), BF16),
            pltpu.SemaphoreType.DMA((4, n)),
            pltpu.SemaphoreType.DMA((4, block_count)),
        ],
        input_output_aliases={1 + len(pieces) + 2 + i: i for i in range(len(held))},
        compiler_params=params(),
        cost_estimate=cost(
            PAIR * row_count * width * 14 * (block + width), 16 * PAIR * row_count * width
        ),
    )(where, *pieces, kv_states, qg_states, *held, *after)
    return result[:4], result[4]


def early_kernel(where, *refs, n, block, chunk):
    pieces, kv_states, qg_states = refs[:n], refs[n], refs[n + 1]
    outs, (held, attention_t, query_t, before_used, sums) = refs[-10:-9], refs[-9:-4]
    wide, stage, in_sems, out_sems = refs[-4:]
    row_count, width = held.shape[2:]
    block_count = row_count // block
    me, z = where[0], where[1]
    copies = place_rows(z, pieces, [(0, K), (0, V), (0, Q)], held, 0, in_sems, n)
    add_shards(me, kv_states, qg_states, sums)
    for c in copies:
        c.wait()
    lower, upper = masks(block)

    def one_block(b):
        at = span(b, block)
        for h in range(PAIR):
            key, value, query = held[K, h, at], held[V, h, at], held[Q, h, at]
            prefix = sums[0, h].astype(BF16)
            before_used[b, h] = prefix
            sums[0, h] += dot(key, value, 0, 0)
            attention_t[b, h] = scores(key, query, upper)
            query_t[b, h] = query.T
            result = dot(query, prefix, 1, 0) + dot(scores(query, key, lower), value, 1, 0)
            wide[0, pl.ds(h, block, stride=PAIR), :] = result / position(
                me * row_count + b * block, block, width
            )
        send_block(wide, stage, outs, out_sems, b, block, chunk, width)

    each(block_count, one_block)
    each(block_count, lambda b: out_copy(stage, outs, out_sems, 0, b, block, chunk).wait())


def late_kernel(where, *refs, n, block, chunk):
    pieces, (held, attention_t, query_t, before_used, sums) = refs[:n], refs[n : n + 5]
    outs = refs[-8:-5]
    grads, wide, stage, in_sems, out_sems = refs[-5:]
    row_count, width = held.shape[2:]
    block_count = row_count // block
    copies = place_rows(where[1], pieces, [(0, 0)], grads, 0, in_sems, n)
    lower, upper = masks(block)
    after = [sums[1, h] for h in range(PAIR)]
    for c in copies:
        c.wait()
    for b in reversed(range(block_count)):
        at = span(b, block)
        turn = wide.at[b % 2]
        for h in range(PAIR):
            key, value, query = held[K, h, at], held[V, h, at], held[Q, h, at]
            grad = grads[0, h, at]
            prefix, suffix = before_used[b, h], after[h].astype(BF16)
            mine = pl.ds(h, block, stride=PAIR)
            grad_scores, grad_scores_t = scores(grad, value, lower), scores(value, grad, upper)
            turn[0, mine, :] = dot(grad, prefix, 1, 1) + dot(grad_scores, key, 1, 0)
            turn[1, mine, :] = dot(value, suffix, 1, 1) + dot(grad_scores_t, query, 1, 0)
            turn[2, mine, :] = dot(key, suffix, 1, 0) + dot(attention_t[b, h], grad, 1, 0)
            if b:
                after[h] = after[h] + dot(query_t[b, h], grad, 1, 0)
        send_block(turn, stage, outs, out_sems, b, block, chunk, width)
    for b in range(block_count):
        for i in range(3):
            out_copy(stage, outs, out_sems, i, b, block, chunk).wait()


def last_chunk(where, kvq, g, kv_states, qg_states, outs, chunk, pair_count, after):
    n = len(kvq)
    _, _, rows, width = kvq[0].shape
    row_count = n * rows
    block = min(BLOCK, row_count)
    block_count = row_count // block
    whole = jax.ShapeDtypeStruct((row_count, pair_count, PAIR, width), BF16)
    held = [] if outs is None else list(outs)
    kept = [
        jax.ShapeDtypeStruct((3, PAIR, row_count, width), BF16),
        jax.ShapeDtypeStruct((block_count, PAIR, block, block), BF16),
        jax.ShapeDtypeStruct((block_count, PAIR, width, block), BF16),
        jax.ShapeDtypeStruct((block_count, PAIR, width, width), BF16),
        jax.ShapeDtypeStruct((2, PAIR, width, width), F32),
    ]
    flops = PAIR * row_count * width * (block + width)
    early = pl.pallas_call(
        functools.partial(early_kernel, n=n, block=block, chunk=chunk),
        in_specs=[SMEM] + [ANY] * n + [VMEM] * 2 + [HBM] * len(held[:1]) + [ANY] * len(after),
        out_specs=[HBM] + [VMEM] * 5,
        out_shape=[whole] + kept,
        scratch_shapes=[
            pltpu.VMEM((1, block * PAIR, width), F32),
            pltpu.VMEM((1, row_count, PAIR, width), BF16),
            pltpu.SemaphoreType.DMA((3, n)),
            pltpu.SemaphoreType.DMA((1, block_count)),
        ],
        input_output_aliases={1 + n + 2: 0} if held else {},
        compiler_params=params(),
        cost_estimate=cost(6 * flops, 8 * PAIR * row_count * width),
    )(where, *kvq, kv_states, qg_states, *held[:1], *after)
    late = pl.pallas_call(
        functools.partial(late_kernel, n=n, block=block, chunk=chunk),
        in_specs=[SMEM] + [ANY] * n + [VMEM] * 5 + [HBM] * len(held[1:]),
        out_specs=[HBM] * 3,
        out_shape=[whole] * 3,
        scratch_shapes=[
            pltpu.VMEM((1, PAIR, row_count, width), BF16),
            pltpu.VMEM((2, 3, block * PAIR, width), F32),
            pltpu.VMEM((3, row_count, PAIR, width), BF16),
            pltpu.SemaphoreType.DMA((1, n)),
            pltpu.SemaphoreType.DMA((3, block_count)),
        ],
        input_output_aliases={1 + n + 5 + i: i for i in range(len(held[1:]))},
        compiler_params=params(),
        cost_estimate=cost(10 * flops, 8 * PAIR * row_count * width),
    )(where, *g, *early[1:], *held[1:])
    return early[0], *late


def plan(per_group):
    last = per_group - 1
    first, second = range(per_group // 2), range(per_group // 2, last)
    units = []
    if first:
        units.append([(K, 0), (V, 0)])
        rest = [(a, c) for c in first for a in range(4)]
        units.append([x for x in rest if x not in units[0]])
    if second:
        units.append([(a, c) for c in second for a in range(4)])
    units += [[(K, last), (V, last), (Q, last)], [(G, last)]]
    return list(first), list(second), [sorted(u, key=lambda x: x[0] == G) for u in units]


def shards(queries, keys_in, values, cotangent):
    n = lax.axis_size("head")
    rows, head_count, width = queries.shape
    pair_count = head_count // PAIR
    per_group = pair_count // n
    last = per_group - 1
    where = jnp.stack([lax.axis_index("seq"), lax.axis_index("head")]).astype(jnp.int32)
    arrays = [
        x.reshape(rows, pair_count, PAIR, width) for x in (keys_in, values, queries, cotangent)
    ]
    first, second, units = plan(per_group)
    sent, arrived = [], []
    for i, items in enumerate(units):
        after = arrived[i - 2][1:] if i >= 2 else [s[0] for s in sent]
        sent.append(pack(where, arrays, items, n, after))
        arrived.append(exchange(sent[-1], n))
    ahead = own_rows_states(where, arrays, last, n, sent[1][:1])
    last_states = lax.all_gather(sum_to_group(ahead, n), "seq", axis=0)

    def place(a, chunk):
        u = next(u for u, items in enumerate(units) if (a, chunk) in items)
        return u, units[u].index((a, chunk))

    def batch_states(batch, after):
        sides = [place(a, c) + place(b, c) for c in batch for a, b in ((K, V), (Q, G))]
        used = sorted({u for s in sides for u in (s[0], s[2])})
        sides = [(used.index(u), a, used.index(w), b) for u, a, w, b in sides]
        own = shard_states([arrived[u] for u in used], sides, after)
        return own, lax.all_gather(own, "seq", axis=0)

    def compute(batch, states, chunk, outs, after):
        slots = [place(a, chunk) for a in range(4)]
        used = sorted({u for u, _ in slots})
        at = 2 * PAIR * batch.index(chunk)
        return compute_chunk(
            where,
            [arrived[u] for u in used],
            [(used.index(u), a) for u, a in slots],
            states[:, at : at + PAIR],
            states[:, at + PAIR : at + 2 * PAIR],
            outs,
            chunk,
            per_group,
            after,
        )

    outs = None
    after = []
    if first:
        _, first_states = batch_states(first, sent[min(3, len(sent) - 1)][:1])
        outs, token = compute(first, first_states, first[0], outs, [])
        after = [token]
    if second:
        own, second_states = batch_states(second, after)
        after = [own]
    for chunk in first[1:]:
        outs, token = compute(first, first_states, chunk, outs, after)
        after = [token]
    for chunk in second:
        outs, token = compute(second, second_states, chunk, outs, after)
        after = [token]
    results = last_chunk(
        where,
        arrived[-2],
        arrived[-1],
        last_states[:, :PAIR],
        last_states[:, PAIR:],
        outs,
        last,
        per_group,
        after,
    )
    return tuple(x.reshape(n * rows, per_group * PAIR, width) for x in results)


def solution(mesh):
    rows_spec = P(("seq", "head"), None, None)
    heads_spec = P("seq", "head", None)
    return jax.shard_map(
        shards, mesh=mesh, in_specs=(rows_spec,) * 4, out_specs=(heads_spec,) * 4, check_vma=False
    )
```

```python
import functools

import jax
import jax.numpy as jnp
from jax import lax
from jax.experimental import pallas as pl
from jax.experimental.pallas import tpu as pltpu
from jax.sharding import PartitionSpec as P

BLOCK = 256
PART = 64
OFFSET = 1048576
PAIR = 2
F32 = jnp.float32
BF16 = jnp.bfloat16
ANY = pl.BlockSpec(memory_space=pl.ANY)
VMEM = pl.BlockSpec(memory_space=pltpu.VMEM)
SMEM = pl.BlockSpec(memory_space=pltpu.SMEM)
VMEM_BYTES = 48 * 1024 * 1024


def dot(a, b, ca, cb):
    return lax.dot_general(a, b, (((ca,), (cb,)), ((), ())), preferred_element_type=F32)


def params():
    return pltpu.CompilerParams(vmem_limit_bytes=VMEM_BYTES)


def cost(flops, nbytes):
    return pl.CostEstimate(flops=int(flops), bytes_accessed=int(nbytes), transcendentals=0)


def partner(z, d):
    return z ^ d


def position(first, rows, width):
    index = lax.broadcasted_iota(jnp.int32, (rows, width), 0) + (first + OFFSET + 1)
    return index.astype(F32)


def pack_kernel(where, *refs, n, scales, n_after):
    count = len(scales)
    sources, rest = refs[: count * n], refs[count * n + n_after :]
    outs, wide = rest[:n], rest[n]
    rows, width = outs[0].shape[2:]
    part_rows = wide.shape[0] // PAIR
    first = (where[0] * n + where[1]) * rows

    def one(i, _):
        at = pl.multiple_of(i * part_rows, part_rows)
        for d in range(n):
            for a in range(count):
                both = sources[count * d + a][pl.ds(at, part_rows)]
                wide[...] = both.reshape(PAIR * part_rows, width).astype(F32)
                for h in range(PAIR):
                    part = wide[pl.ds(h, part_rows, stride=PAIR), :]
                    if scales[a]:
                        part = part / position(first + at, part_rows, width)
                    outs[d][a, h, pl.ds(at, part_rows)] = part.astype(BF16)
        return 0

    lax.fori_loop(0, rows // part_rows, one, 0)


def pack(where, arrays, scales, chunk, n, after):
    rows, pair_count, _, width = arrays[0].shape
    per_group = pair_count // n
    count = len(arrays)

    def spec(d):
        return pl.BlockSpec(
            (rows, 1, PAIR, width),
            lambda i, w: (0, partner(w[1], d) * per_group + chunk, 0, 0),
        )

    out = jax.ShapeDtypeStruct((count, PAIR, rows, width), BF16)
    specs = [spec(d) for d in range(n) for _ in arrays] + [ANY] * len(after)
    operands = [x for _ in range(n) for x in arrays] + list(after)
    return pl.pallas_call(
        functools.partial(pack_kernel, n=n, scales=scales, n_after=len(after)),
        grid_spec=pltpu.PrefetchScalarGridSpec(
            num_scalar_prefetch=1,
            grid=(1,),
            in_specs=specs,
            out_specs=[pl.BlockSpec((count, PAIR, rows, width), lambda i, w: (0, 0, 0, 0))] * n,
            scratch_shapes=[pltpu.VMEM((PAIR * min(rows, PART), width), F32)],
        ),
        out_shape=[out] * n,
        compiler_params=params(),
        cost_estimate=cost(0, 4 * count * n * PAIR * rows * width),
    )(where, *operands)


def exchange(pieces, n):
    received = [pieces[0]]
    for d in range(1, n):
        received.append(None)
    for d in reversed(range(1, n)):
        received[d] = lax.ppermute(pieces[d], "head", [(j, j ^ d) for j in range(n)])
    return received


def state_kernel(*refs, n, at):
    for h in range(PAIR):
        total = dot(refs[0][at, h], refs[0][at + 1, h], 0, 0)
        for d in range(1, n):
            total = total + dot(refs[d][at, h], refs[d][at + 1, h], 0, 0)
        refs[n][h] = total.astype(BF16)


def shard_state(pieces, slot):
    n = len(pieces)
    _, _, rows, width = pieces[0].shape
    return pl.pallas_call(
        functools.partial(state_kernel, n=n, at=2 * slot),
        in_specs=[VMEM] * n,
        out_specs=VMEM,
        out_shape=jax.ShapeDtypeStruct((PAIR, width, width), BF16),
        compiler_params=params(),
        cost_estimate=cost(2 * n * PAIR * rows * width * width, 4 * n * PAIR * rows * width),
    )(*pieces)


def chunk_kernel(where, *refs, n, block):
    kv_pieces, qg_pieces = refs[:n], refs[n : 2 * n]
    kv_states, qg_states = refs[2 * n], refs[2 * n + 1]
    result, grad_query, grad_key, grad_value = refs[-8:-4]
    left, right, wide, used = refs[-4:]
    shard_count = kv_states.shape[0]
    rows, width = kv_pieces[0].shape[2:]
    row_count = n * rows
    block_count = row_count // block
    me, z = where[0], where[1]
    for d in range(n):
        start = pl.multiple_of(partner(z, d) * rows, rows)
        left[:, :, pl.ds(start, rows), :] = kv_pieces[d][...]
        right[:, :, pl.ds(start, rows), :] = qg_pieces[d][...]
    causal = lax.broadcasted_iota(jnp.int32, (block, block), 0) >= lax.broadcasted_iota(
        jnp.int32, (block, block), 1
    )

    def scores(a, b):
        return jnp.where(causal, dot(a, b, 1, 1), 0.0).astype(BF16)

    for h in range(PAIR):
        before = jnp.zeros((width, width), F32)
        after = jnp.zeros((width, width), F32)
        for j in range(shard_count):
            before = before + jnp.where(j < me, kv_states[j, h].astype(F32), 0.0)
            after = after + jnp.where(j > me, qg_states[j, h].astype(F32), 0.0)
        for b in reversed(range(block_count)):
            span = pl.ds(b * block, block)
            used[b] = after.astype(BF16)
            if b:
                after = after + dot(right[0, h, span], right[1, h, span], 0, 0)
        for b in range(block_count):
            span = pl.ds(b * block, block)
            key, value = left[0, h, span], left[1, h, span]
            query, grad = right[0, h, span], right[1, h, span]
            prefix, suffix = before.astype(BF16), used[b]
            attention, grad_scores = scores(query, key), scores(grad, value)
            out_rows = pl.ds(b * block * PAIR + h, block, stride=PAIR)
            wide[0, out_rows, :] = (
                dot(query, prefix, 1, 0) + dot(attention, value, 1, 0)
            ) / position(me * row_count + b * block, block, width)
            wide[1, out_rows, :] = dot(grad, prefix, 1, 1) + dot(grad_scores, key, 1, 0)
            wide[2, out_rows, :] = dot(value, suffix, 1, 1) + dot(grad_scores, query, 0, 0)
            wide[3, out_rows, :] = dot(key, suffix, 1, 0) + dot(attention, grad, 0, 0)
            if b + 1 < block_count:
                before = before + dot(key, value, 0, 0)
    for i, out in enumerate((result, grad_query, grad_key, grad_value)):
        out[...] = wide[i].astype(BF16).reshape(row_count, 1, PAIR, width)


def compute_chunk(where, kv, qg, slots, kv_states, qg_states, outs, chunk, pair_count):
    n = len(kv)
    _, _, rows, width = kv[0].shape
    row_count = n * rows
    block = min(BLOCK, row_count)
    whole = jax.ShapeDtypeStruct((row_count, pair_count, PAIR, width), BF16)
    pieces = [
        pl.BlockSpec((2, PAIR, rows, width), lambda i, w, slot=slot: (slot, 0, 0, 0))
        for slot in slots
        for _ in range(n)
    ]
    state = pl.BlockSpec(kv_states.shape, lambda i, w: (0, 0, 0, 0))
    held = [] if outs is None else list(outs)
    first_held = 1 + 2 * n + 2
    flops = PAIR * row_count * width * (12 * block + 12 * width)
    return pl.pallas_call(
        functools.partial(chunk_kernel, n=n, block=block),
        grid_spec=pltpu.PrefetchScalarGridSpec(
            num_scalar_prefetch=1,
            grid=(1,),
            in_specs=pieces + [state] * 2 + [ANY] * len(held),
            out_specs=[
                pl.BlockSpec((row_count, 1, PAIR, width), lambda i, w: (0, chunk, 0, 0))
            ]
            * 4,
            scratch_shapes=[
                pltpu.VMEM((2, PAIR, row_count, width), BF16),
                pltpu.VMEM((2, PAIR, row_count, width), BF16),
                pltpu.VMEM((4, row_count * PAIR, width), F32),
                pltpu.VMEM((row_count // block, width, width), BF16),
            ],
        ),
        out_shape=[whole] * 4,
        input_output_aliases={first_held + i: i for i in range(len(held))},
        compiler_params=params(),
        cost_estimate=cost(flops, 16 * PAIR * row_count * width),
    )(where, *kv, *qg, kv_states, qg_states, *held)


def shards(queries, keys_in, values, cotangent):
    n = lax.axis_size("head")
    rows, head_count, width = queries.shape
    pair_count = head_count // PAIR
    per_group = pair_count // n
    where = jnp.stack([lax.axis_index("seq"), lax.axis_index("head")]).astype(jnp.int32)

    def paired(x):
        return x.reshape(rows, pair_count, PAIR, width)

    queries, keys_in, values, cotangent = map(paired, (queries, keys_in, values, cotangent))
    both = {"kv": ((keys_in, values), (False, False)), "qg": ((queries, cotangent), (False, True))}
    units = []
    for chunk in range(per_group):
        sides = [("kv", chunk), ("qg", chunk)]
        units += [[x] for x in sides]
    arrived, received = {}, []
    for i, unit in enumerate(units):
        after = received[i - 2][1:] if i >= 2 else []
        arrays = [x for side, _ in unit for x in both[side][0]]
        scales = [x for side, _ in unit for x in both[side][1]]
        received.append(exchange(pack(where, arrays, scales, unit[0][1], n, after), n))
        for slot, key in enumerate(unit):
            arrived[key] = received[i], slot
    outs = None
    for chunk in range(per_group):
        (kv, kv_slot), (qg, qg_slot) = arrived["kv", chunk], arrived["qg", chunk]
        kv_states = lax.all_gather(shard_state(kv, kv_slot), "seq", axis=0)
        qg_states = lax.all_gather(shard_state(qg, qg_slot), "seq", axis=0)
        slots = (kv_slot, qg_slot)
        outs = compute_chunk(
            where, kv, qg, slots, kv_states, qg_states, outs, chunk, per_group
        )
    return tuple(x.reshape(n * rows, per_group * PAIR, width) for x in outs)


def solution(mesh):
    rows_spec = P(("seq", "head"), None, None)
    heads_spec = P("seq", "head", None)
    return jax.shard_map(
        shards, mesh=mesh, in_specs=(rows_spec,) * 4, out_specs=(heads_spec,) * 4, check_vma=False
    )
```
